32 devices in a mesh: patch: 8 (over z, x), frame: 4 (over y, core).
Axes of the slice: x: 2, y: 2, z: 4, core: 2. Of those that a mesh axis runs over, the one named last changes fastest.
Arguments:
- screens: float32 [2, 512, 4096], P(None, 'patch'), may hold values from -6 to 6
- row_offsets: int32 [4, 2, 8], replicated, may hold values from 0 to 256
- col_offsets: int32 [4, 2, 8], replicated, may hold values from 0 to 3840
- amplitude: float32 [256, 256], replicated, may hold values from 0.5 to 1.5
- object_strip: float32 [384, 2048], P(None, 'patch'), may hold values from 0.5 to 1.5
- observed: float32 [4, 256, 2048], P('frame', None, 'patch'), may hold values from 0.5 to 1.5
Outputs:
- screen_grad: float32 [2, 512, 4096], P(None, 'patch', 'frame')
The draws below stay inside these ranges and needn't reach their ends.
All inputs are finite; a program needn't handle non-finite values.
Results may differ from the reference program's by a relative error of at most 0.0003.
Values sent between devices are 32-bit elements; how exact they have to be, the bound alone decides.
A program may use at most 128 MiB of HBM per device.

```python
import jax
import jax.numpy as jnp
from jax import lax

CORE = 256
HALO = 64
WIN = 256
SPAN = 384
LAYERS = 2
SCOLS = 4096
FRAMES = 4
PATCHES = 8
SCREEN_ROWS = 512


def draw_row_offsets(key, part):
    first_key, second_key = jax.random.split(jax.random.fold_in(key, 11))
    highest = SCREEN_ROWS - WIN
    jitter_span = WIN // 2
    base_rows = jax.random.randint(first_key, (FRAMES, LAYERS, 1), 0, highest - jitter_span + 1)
    jitter = jax.random.randint(second_key, (FRAMES, LAYERS, PATCHES), 0, jitter_span + 1)
    rows_all = base_rows + jitter
    rows_all = rows_all.at[0, 0, 0].set(0).at[FRAMES - 1, LAYERS - 1, PATCHES - 1].set(highest)
    return rows_all.astype(jnp.int32)


def draw_col_offsets(key, part):
    first_key, second_key = jax.random.split(jax.random.fold_in(key, 23))
    highest = SCOLS - WIN
    layer_step = jax.random.randint(first_key, (1, LAYERS, 1), 0, highest // PATCHES + 1)
    raw_base = jax.random.randint(second_key, (FRAMES, LAYERS, 1), 0, 1 << 20)
    base_cols = raw_base % (highest - layer_step * (PATCHES - 1) + 1)
    cols_all = base_cols + layer_step * jnp.arange(PATCHES, dtype=jnp.int32)[None, None, :]
    cols_all = cols_all.at[0, 0, 0].set(0).at[FRAMES - 1, LAYERS - 1, PATCHES - 1].set(highest)
    return cols_all.astype(jnp.int32)


def shard_levels(stream_key, shape, cuts, least, top_value):
    loudness = 1.0
    for dim, shards_of in cuts:
        steps = jax.random.uniform(jax.random.fold_in(jax.random.fold_in(stream_key, 6), dim), (shards_of,), jnp.float32, least / len(cuts), top_value / len(cuts))
        loudness = loudness * jnp.repeat(jnp.exp(steps), shape[dim] // shards_of).reshape((-1,) + (1,) * (len(shape) - 1 - dim))
    return loudness


def gaussian(rng, dims, scale, bound, cuts=(), kind=jnp.bfloat16):
    entries = jax.random.normal(rng, dims, jnp.float32) * scale
    if len(cuts) > 0:
        entries = shard_levels(rng, dims, cuts, -0.22, 0.18) * entries
    return jnp.clip(entries, min=-bound, max=bound).astype(kind)


def setup_inputs(seed: int = 0) -> dict:
    keys = jax.random.split(jax.random.key(seed), 7)
    return {
        "screens": gaussian(keys[0], (LAYERS, SCREEN_ROWS, SCOLS), 1.0, 6.0, ((1, 8),), jnp.float32),
        "row_offsets": draw_row_offsets(jax.random.fold_in(keys[6], 71), 0),
        "col_offsets": draw_col_offsets(jax.random.fold_in(keys[6], 71), 0),
        "amplitude": jnp.clip(jax.random.uniform(keys[3], (WIN, WIN), jnp.float32, 0.5, 1.5), 0.5, 1.5),
        "object_strip": jnp.clip(0.5 + 1.0 * jax.random.uniform(keys[4], (SPAN, PATCHES * CORE), jnp.float32) ** shard_levels(keys[4], (SPAN, PATCHES * CORE), ((1, 8),), -0.2, 0.2), 0.5, 1.5),
        "observed": jnp.clip(0.5 + 1.0 * jax.random.uniform(keys[5], (FRAMES, CORE, PATCHES * CORE), jnp.float32) ** shard_levels(keys[5], (FRAMES, CORE, PATCHES * CORE), ((0, 4), (2, 8)), -0.2, 0.2), 0.5, 1.5),
    }


def pair_gradient(phases, window, target, amplitude):
    extent = window.shape[0]
    win_size = phases.shape[0]
    core_size = target.shape[0]
    margin = (extent - core_size) // 2
    inverse_total = 1.0 / (extent * extent * jnp.sum(amplitude * amplitude))
    pupil_field = amplitude * jnp.exp(1j * phases)
    padded = jnp.zeros((extent, extent), pupil_field.dtype).at[:win_size, :win_size].set(pupil_field)
    far_field = jnp.fft.fft2(padded)
    spread = (jnp.real(far_field) ** 2 + jnp.imag(far_field) ** 2) * inverse_total
    object_spec = jnp.fft.fft2(window)
    model_image = jnp.real(jnp.fft.ifft2(jnp.fft.fft2(spread) * object_spec))
    residual = (model_image[margin:margin + core_size, margin:margin + core_size] - target) * (win_size * extent / core_size)
    model_grad = jnp.zeros((extent, extent), residual.dtype).at[margin:margin + core_size, margin:margin + core_size].set(residual)
    spread_grad = jnp.real(jnp.fft.ifft2(jnp.fft.fft2(model_grad) * jnp.conj(object_spec)))
    backward = (extent * extent) * jnp.fft.ifft2(far_field * spread_grad)[:win_size, :win_size]
    return 2.0 * inverse_total * (jnp.real(pupil_field) * jnp.imag(backward) - jnp.imag(pupil_field) * jnp.real(backward))


def reference(screens, row_offsets, col_offsets, amplitude, object_strip, observed):
    extent = object_strip.shape[0]
    padded_object = jnp.pad(object_strip, ((0, 0), (HALO, HALO)))

    def single(position):
        position = position.astype(jnp.int32)
        frame_id = position // PATCHES
        patch_id = position % PATCHES
        phases = jnp.zeros((WIN, WIN), screens.dtype)
        for layer_id in range(LAYERS):
            phases = phases + lax.dynamic_slice(screens[layer_id], (row_offsets[frame_id, layer_id, patch_id], col_offsets[frame_id, layer_id, patch_id]), (WIN, WIN))
        begin_col = (patch_id * CORE).astype(jnp.int32)
        window = lax.dynamic_slice(padded_object, (jnp.int32(0), begin_col), (extent, extent))
        target = lax.dynamic_slice(observed[frame_id], (jnp.int32(0), begin_col), (CORE, CORE))
        return pair_gradient(phases, window, target, amplitude)

    gradients = lax.map(single, jnp.arange(FRAMES * PATCHES, dtype=jnp.int32))

    def accumulate(position, running):
        position = position.astype(jnp.int32)
        frame_id = position // PATCHES
        patch_id = position % PATCHES
        for layer_id in range(LAYERS):
            corner = (jnp.int32(layer_id), row_offsets[frame_id, layer_id, patch_id], col_offsets[frame_id, layer_id, patch_id])
            current = lax.dynamic_slice(running, corner, (1, WIN, WIN))
            running = lax.dynamic_update_slice(running, current + gradients[position][None], corner)
        return running

    return lax.fori_loop(0, FRAMES * PATCHES, accumulate, jnp.zeros_like(screens))
```

```python
import functools

import jax
import jax.numpy as jnp
import numpy as np
from jax import lax
from jax.experimental import pallas as pl
from jax.experimental.pallas import tpu as pltpu
from jax.sharding import PartitionSpec as P

CORE = 256
HALO = 64
LANES = 128
SUBLANES = 8
RADIX = 3
HALF_ROOT3 = float(np.sqrt(3.0) / 2)
VMEM_LIMIT = 48 * 1024 * 1024
VMEM_SPEC = pl.BlockSpec(memory_space=pltpu.VMEM)
SMEM_SPEC = pl.BlockSpec(memory_space=pltpu.SMEM)


def split(values):
    high = values.astype(jnp.bfloat16)
    return high, (values - high.astype(jnp.float32)).astype(jnp.bfloat16)


def product(left, right):
    dot = functools.partial(jnp.dot, preferred_element_type=jnp.float32)
    return dot(left[0], right[1]) + dot(left[1], right[0]) + dot(left[0], right[0])


def left_product(matrix, values):
    return product(matrix, split(values))


def right_product(values, matrix):
    return product(split(values), matrix)


def transform_matrices(extent):
    part = extent // RADIX
    index = np.arange(part)
    angles = (pow(RADIX, -1, part) * index[:, None] * index[None, :] % part) * (2 * np.pi / part)
    cosine, sine = np.cos(angles), np.sin(angles)
    forward = np.block([[cosine, sine], [-sine, cosine]]).astype(np.float32)
    arrays = []
    for matrix in (forward, forward.T):
        high = matrix.astype(jnp.bfloat16)
        low = (matrix - high.astype(np.float32)).astype(jnp.bfloat16)
        arrays += [high, low]
    return arrays


def residue(shape, axis):
    return lax.broadcasted_iota(jnp.int32, shape, axis) % RADIX


def pick(blocks, which):
    result = blocks[0]
    for number in range(1, RADIX):
        result = jnp.where(which == number, blocks[number], result)
    return result


def to_residues(blocks, axis):
    like = blocks[0]
    blocks = list(blocks) + [jnp.zeros_like(like)] * (RADIX - len(blocks))
    rest = residue(like.shape, axis)
    part = like.shape[axis]
    inverse = pow(part, -1, RADIX)
    return [pick(blocks, (inverse * (j + 2 * rest)) % RADIX) for j in range(RADIX)]


def to_natural(blocks, axis, count):
    rest = residue(blocks[0].shape, axis)
    part = blocks[0].shape[axis]
    return [pick(blocks, (part * j + rest) % RADIX) for j in range(count)]


def blocks_of(values, axis):
    count = values.shape[axis] // LANES
    return [lax.slice_in_dim(values, j * LANES, (j + 1) * LANES, axis=axis) for j in range(count)]


def butterfly(re, im, sign):
    sum_re, sum_im = re[1] + re[2], im[1] + im[2]
    mid_re, mid_im = re[0] - 0.5 * sum_re, im[0] - 0.5 * sum_im
    turn_re = (sign * HALF_ROOT3) * (re[1] - re[2])
    turn_im = (sign * HALF_ROOT3) * (im[1] - im[2])
    return (
        [re[0] + sum_re, mid_re - turn_im, mid_re + turn_im],
        [im[0] + sum_im, mid_im + turn_re, mid_im - turn_re],
    )


def halves(values, axis):
    size = values.shape[axis] // 2
    return (
        lax.slice_in_dim(values, 0, size, axis=axis),
        lax.slice_in_dim(values, size, 2 * size, axis=axis),
    )


def columns_forward(re, im, turned):
    re, im = butterfly(re, im, 1.0)
    pairs = [
        halves(right_product(jnp.concatenate([a, b], axis=1), turned), 1) for a, b in zip(re, im)
    ]
    return jnp.concatenate([p[0] for p in pairs], axis=1), jnp.concatenate(
        [p[1] for p in pairs], axis=1
    )


def columns_inverse(re, im, plain):
    pairs = [
        halves(right_product(jnp.concatenate([a, b], axis=1), plain), 1)
        for a, b in zip(blocks_of(re, 1), blocks_of(im, 1))
    ]
    return butterfly([p[0] for p in pairs], [p[1] for p in pairs], -1.0)


def rows_forward(re, im, plain):
    re, im = butterfly(re, im, 1.0)
    pairs = [
        halves(left_product(plain, jnp.concatenate([a, b], axis=0)), 0) for a, b in zip(re, im)
    ]
    return jnp.concatenate([p[0] for p in pairs], axis=0), jnp.concatenate(
        [p[1] for p in pairs], axis=0
    )


def rows_inverse(re, im, turned):
    pairs = [
        halves(left_product(turned, jnp.concatenate([a, b], axis=0)), 0)
        for a, b in zip(blocks_of(re, 0), blocks_of(im, 0))
    ]
    return butterfly([p[0] for p in pairs], [p[1] for p in pairs], -1.0)


def rows_forward_real(blocks, plain):
    part = blocks[0].shape[0]
    total = blocks[1] + blocks[2]
    narrow = (plain[0][:, :part], plain[1][:, :part])
    first = halves(left_product(narrow, blocks[0] + total), 0)
    turned = jnp.concatenate(
        [blocks[0] - 0.5 * total, HALF_ROOT3 * (blocks[1] - blocks[2])], axis=0
    )
    second = halves(left_product(plain, turned), 0)
    return jnp.concatenate([first[0], second[0]], axis=0), jnp.concatenate(
        [first[1], second[1]], axis=0
    )


def rows_inverse_real(re, im, turned):
    re, im = blocks_of(re, 0), blocks_of(im, 0)
    part = re[0].shape[0]
    short = (turned[0][:part], turned[1][:part])
    base = left_product(short, jnp.concatenate([re[0], im[0]], axis=0))
    pair_re, pair_im = halves(left_product(turned, jnp.concatenate([re[1], im[1]], axis=0)), 0)
    near, far = base - pair_re, (2 * HALF_ROOT3) * pair_im
    return [base + 2.0 * pair_re, near + far, near - far]


def sine_cosine(angle):
    quarter = jnp.floor(angle * np.float32(2 / np.pi) + 0.5)
    rest = angle - quarter * np.float32(1.5703125)
    rest = rest - quarter * np.float32(4.837512969970703125e-4)
    rest = rest - quarter * np.float32(7.549789948768648e-8)
    square = rest * rest
    sine = rest + rest * square * (
        -1.6666654611e-1 + square * (8.3321608736e-3 - 1.9515295891e-4 * square)
    )
    cosine = (
        1.0
        - 0.5 * square
        + square
        * square
        * (4.166664568298827e-2 + square * (-1.388731625493765e-3 + 2.443315711809948e-5 * square))
    )
    turn = quarter.astype(jnp.int32) & 3
    swap = (turn & 1) == 1
    out_sine = jnp.where(swap, cosine, sine)
    out_cosine = jnp.where(swap, sine, cosine)
    out_sine = jnp.where(turn >= 2, -out_sine, out_sine)
    out_cosine = jnp.where((turn == 1) | (turn == 2), -out_cosine, out_cosine)
    return out_sine, out_cosine


def object_kernel(window_ref, fh, fl, th, tl, re_ref, im_ref):
    plain, turned = (fh[...], fl[...]), (th[...], tl[...])
    extent = window_ref.shape[0]
    values = window_ref[...] * (1.0 / (extent * extent))
    re, im = rows_forward_real(to_residues(blocks_of(values, 0), 0), plain)
    re, im = columns_forward(
        to_residues(blocks_of(re, 1), 1), to_residues(blocks_of(im, 1), 1), turned
    )
    re_ref[...] = re
    im_ref[...] = im


def pair_gradient(phases, target, amplitude, object_re, object_im, plain, turned):
    win_size = phases.shape[0]
    extent = object_re.shape[1]
    naturals = win_size // LANES
    inverse_total = 1.0 / (extent * extent * jnp.sum(amplitude * amplitude))
    sine, cosine = sine_cosine(phases)
    pupil_re, pupil_im = amplitude * cosine, amplitude * sine

    def parts(values, axis):
        return to_residues(blocks_of(values, axis), axis)

    re, im = rows_forward(parts(pupil_re, 0), parts(pupil_im, 0), plain)
    far_re, far_im = columns_forward(parts(re, 1), parts(im, 1), turned)
    spread = (far_re * far_re + far_im * far_im) * inverse_total
    re, im = rows_forward_real(blocks_of(spread, 0), plain)
    re, im = columns_forward(blocks_of(re, 1), blocks_of(im, 1), turned)
    re, im = re * object_re - im * object_im, re * object_im + im * object_re
    re, im = columns_inverse(re, im, plain)
    re = jnp.concatenate(to_natural(re, 1, naturals), axis=1)
    im = jnp.concatenate(to_natural(im, 1, naturals), axis=1)
    model = jnp.concatenate(to_natural(rows_inverse_real(re, im, turned), 0, naturals), axis=0)
    residual = (model - target) * (win_size * extent / target.shape[0])
    re, im = rows_forward_real(parts(residual, 0), plain)
    re, im = columns_forward(parts(re, 1), parts(im, 1), turned)
    re, im = re * object_re + im * object_im, im * object_re - re * object_im
    re, im = columns_inverse(re, im, plain)
    spread_grad = jnp.concatenate(
        rows_inverse_real(jnp.concatenate(re, axis=1), jnp.concatenate(im, axis=1), turned), axis=0
    )
    re, im = columns_inverse(far_re * spread_grad, far_im * spread_grad, plain)
    re = jnp.concatenate(to_natural(re, 1, naturals), axis=1)
    im = jnp.concatenate(to_natural(im, 1, naturals), axis=1)
    re, im = rows_inverse(re, im, turned)
    back_re = jnp.concatenate(to_natural(re, 0, naturals), axis=0)
    back_im = jnp.concatenate(to_natural(im, 0, naturals), axis=0)
    return 2.0 * inverse_total * (pupil_re * back_im - pupil_im * back_re)


def aligned(offset, unit, size, width):
    begin = jnp.minimum((offset // unit) * unit, size - width)
    return pl.multiple_of(begin, unit), offset - begin


def patch_kernel(
    rows_ref, bands_ref, target_ref, amplitude_ref, ore_ref, oim_ref, fh, fl, th, tl, out_ref, sheet
):
    count, layers, tile, win_size = bands_ref.shape
    reach = win_size + SUBLANES
    plain, turned = (fh[...], fl[...]), (th[...], tl[...])
    phases = None
    corners = []
    for layer in range(layers):
        for holder in range(count):
            sheet[layer, pl.ds(holder * tile, tile), :] = bands_ref[holder, layer]
        begin, shift = aligned(rows_ref[layer], SUBLANES, count * tile, reach)
        corners.append((begin, shift))
        rows = sheet[layer, pl.ds(begin, reach), :]
        rows = pltpu.roll(rows, jnp.where(shift == 0, 0, reach - shift), 0)[:win_size]
        phases = rows if phases is None else phases + rows
    gradient = pair_gradient(
        phases, target_ref[...], amplitude_ref[...], ore_ref[...], oim_ref[...], plain, turned
    )
    padded = jnp.concatenate([gradient, jnp.zeros((SUBLANES, win_size), jnp.float32)], axis=0)
    for layer in range(layers):
        begin, shift = corners[layer]
        sheet[layer] = jnp.zeros((count * tile, win_size), jnp.float32)
        sheet[layer, pl.ds(begin, reach), :] = pltpu.roll(padded, shift, 0)
        for holder in range(count):
            out_ref[holder, layer] = sheet[layer, pl.ds(holder * tile, tile), :]


def cut_kernel(cols_ref, screens_ref, out_ref):
    layers, tile, screen_cols = screens_ref.shape
    count, _, _, win_size = out_ref.shape
    reach = win_size + LANES

    @pl.loop(0, count)
    def _(patch):
        for layer in range(layers):
            begin, shift = aligned(cols_ref[layer, patch], LANES, screen_cols, reach)
            cells = screens_ref[layer, :, pl.ds(begin, reach)]
            cells = pltpu.roll(cells, jnp.where(shift == 0, 0, reach - shift), 1)
            out_ref[patch, layer] = cells[:, :win_size]


def add_kernel(cols_ref, frame_ref, bands_ref, keep_ref, send_ref, sheet):
    count, layers, tile, win_size = bands_ref.shape
    screen_cols = sheet.shape[2]
    reach = win_size + LANES
    chunks, _, _, width = keep_ref.shape
    sheet[...] = jnp.zeros_like(sheet)

    @pl.loop(0, count)
    def _(patch):
        for layer in range(layers):
            begin, shift = aligned(cols_ref[layer, patch], LANES, screen_cols, reach)
            cells = jnp.concatenate(
                [bands_ref[patch, layer], jnp.zeros((tile, LANES), jnp.float32)], axis=1
            )
            sheet[layer, :, pl.ds(begin, reach)] += pltpu.roll(cells, shift, 1)

    bit = frame_ref[0] & 1
    for chunk in range(chunks):
        for ref, low in ((keep_ref, bit), (send_ref, 1 - bit)):
            begin = pl.multiple_of((2 * chunk + low) * width, LANES)
            for layer in range(layers):
                ref[chunk, layer] = sheet[layer, :, pl.ds(begin, width)]


def call(kernel, out_shape, specs, scratch=(), flops=0, moved=0):
    return pl.pallas_call(
        kernel,
        out_shape=out_shape,
        in_specs=specs,
        out_specs=jax.tree.map(lambda _: VMEM_SPEC, out_shape),
        scratch_shapes=list(scratch),
        cost_estimate=pl.CostEstimate(flops=flops, bytes_accessed=moved, transcendentals=0),
        compiler_params=pltpu.CompilerParams(vmem_limit_bytes=VMEM_LIMIT),
    )


def frame_total(keep, send, frame_id):
    count = lax.axis_size("frame")
    step = 1
    while True:
        received = lax.ppermute(send, "frame", [(i, i ^ step) for i in range(count)])
        total = keep + received
        if total.shape[0] == 1:
            return total[0]
        step *= 2
        bit = (frame_id // step) % 2
        pairs = total.reshape((total.shape[0] // 2, 2) + total.shape[1:])
        keep = lax.dynamic_index_in_dim(pairs, bit, 1, keepdims=False)
        send = lax.dynamic_index_in_dim(pairs, 1 - bit, 1, keepdims=False)


def body(screens, row_offsets, col_offsets, amplitude, object_strip, observed):
    patch_count = lax.axis_size("patch")
    frame_count = lax.axis_size("frame")
    place = lax.axis_index("patch")
    frame_id = lax.axis_index("frame")
    layers, tile, screen_cols = screens.shape
    win_size = amplitude.shape[0]
    extent = object_strip.shape[0]
    width = screen_cols // frame_count
    float_of = lambda *shape: jax.ShapeDtypeStruct(shape, jnp.float32)
    matrices = [jnp.asarray(m) for m in transform_matrices(extent)]
    cols = lax.dynamic_index_in_dim(col_offsets, frame_id, 0, keepdims=False)
    rows = lax.dynamic_slice(row_offsets, (frame_id, 0, place), (1, layers, 1)).reshape(layers)

    bands = call(
        cut_kernel,
        float_of(patch_count, layers, tile, win_size),
        [SMEM_SPEC, VMEM_SPEC],
        moved=2 * screens.size * 4,
    )(cols, screens)
    received = lax.all_to_all(bands, "patch", split_axis=0, concat_axis=0, tiled=True)

    ends = patch_count - 1
    head = lax.slice_in_dim(object_strip, 0, HALO, axis=1)
    tail = lax.slice_in_dim(object_strip, object_strip.shape[1] - HALO, None, axis=1)
    right = lax.ppermute(head, "patch", [(i + 1, i) for i in range(ends)])
    left = lax.ppermute(tail, "patch", [(i, i + 1) for i in range(ends)])
    window = jnp.concatenate([object_strip, right, left], axis=1)
    window = jnp.concatenate([window[HALO:], window[:HALO]], axis=0)
    spectrum = float_of(2 * (extent // RADIX), extent)
    object_re, object_im = call(
        object_kernel, (spectrum, spectrum), [VMEM_SPEC] * 5, flops=3 * 10**9, moved=2 * 10**6
    )(window, *matrices)

    outgoing = call(
        patch_kernel,
        float_of(patch_count, layers, tile, win_size),
        [SMEM_SPEC] + [VMEM_SPEC] * 9,
        scratch=[pltpu.VMEM((layers, patch_count * tile, win_size), jnp.float32)],
        flops=10**10,
        moved=8 * 10**6,
    )(rows, received, observed[0], amplitude, object_re, object_im, *matrices)
    returned = lax.all_to_all(outgoing, "patch", split_axis=0, concat_axis=0, tiled=True)

    pieces = float_of(frame_count // 2, layers, tile, width)
    keep, send = call(
        add_kernel,
        (pieces, pieces),
        [SMEM_SPEC, SMEM_SPEC, VMEM_SPEC],
        scratch=[pltpu.VMEM((layers, tile, screen_cols), jnp.float32)],
        moved=8 * 10**6,
    )(cols, frame_id.reshape(1).astype(jnp.int32), returned)
    return frame_total(keep, send, frame_id)


def solution(mesh):
    in_specs = (P(None, "patch", None), P(), P(), P(), P(None, "patch"), P("frame", None, "patch"))
    out_specs = P(None, "patch", "frame")
    return jax.shard_map(body, mesh=mesh, in_specs=in_specs, out_specs=out_specs, check_vma=False)
```

```python
import functools

import jax
import jax.numpy as jnp
import numpy as np
from jax import lax
from jax.experimental import pallas as pl
from jax.experimental.pallas import tpu as pltpu
from jax.sharding import PartitionSpec as P

CORE = 256
HALO = 64
LANES = 128
SUBLANES = 8
RADIX = 3
HALF_ROOT3 = float(np.sqrt(3.0) / 2)
VMEM_LIMIT = 48 * 1024 * 1024
VMEM_SPEC = pl.BlockSpec(memory_space=pltpu.VMEM)
SMEM_SPEC = pl.BlockSpec(memory_space=pltpu.SMEM)


def split(values):
    high = values.astype(jnp.bfloat16)
    return high, (values - high.astype(jnp.float32)).astype(jnp.bfloat16)


def product(left, right):
    dot = functools.partial(jnp.dot, preferred_element_type=jnp.float32)
    return dot(left[0], right[1]) + dot(left[1], right[0]) + dot(left[0], right[0])


def left_product(matrix, values):
    return product(matrix, split(values))


def right_product(values, matrix):
    return product(split(values), matrix)


def transform_matrices(extent):
    part = extent // RADIX
    index = np.arange(part)
    angles = (pow(RADIX, -1, part) * index[:, None] * index[None, :] % part) * (2 * np.pi / part)
    cosine, sine = np.cos(angles), np.sin(angles)
    forward = np.block([[cosine, sine], [-sine, cosine]]).astype(np.float32)
    arrays = []
    for matrix in (forward, forward.T):
        high = matrix.astype(jnp.bfloat16)
        low = (matrix - high.astype(np.float32)).astype(jnp.bfloat16)
        arrays += [high, low]
    return arrays


def residue(shape, axis):
    return lax.broadcasted_iota(jnp.int32, shape, axis) % RADIX


def pick(blocks, which):
    result = blocks[0]
    for number in range(1, RADIX):
        result = jnp.where(which == number, blocks[number], result)
    return result


def to_residues(blocks, axis):
    like = blocks[0]
    blocks = list(blocks) + [jnp.zeros_like(like)] * (RADIX - len(blocks))
    rest = residue(like.shape, axis)
    part = like.shape[axis]
    inverse = pow(part, -1, RADIX)
    return [pick(blocks, (inverse * (j + 2 * rest)) % RADIX) for j in range(RADIX)]


def to_natural(blocks, axis, count):
    rest = residue(blocks[0].shape, axis)
    part = blocks[0].shape[axis]
    return [pick(blocks, (part * j + rest) % RADIX) for j in range(count)]


def blocks_of(values, axis):
    count = values.shape[axis] // LANES
    return [lax.slice_in_dim(values, j * LANES, (j + 1) * LANES, axis=axis) for j in range(count)]


def butterfly(re, im, sign):
    sum_re, sum_im = re[1] + re[2], im[1] + im[2]
    mid_re, mid_im = re[0] - 0.5 * sum_re, im[0] - 0.5 * sum_im
    turn_re = (sign * HALF_ROOT3) * (re[1] - re[2])
    turn_im = (sign * HALF_ROOT3) * (im[1] - im[2])
    return (
        [re[0] + sum_re, mid_re - turn_im, mid_re + turn_im],
        [im[0] + sum_im, mid_im + turn_re, mid_im - turn_re],
    )


def halves(values, axis):
    size = values.shape[axis] // 2
    return (
        lax.slice_in_dim(values, 0, size, axis=axis),
        lax.slice_in_dim(values, size, 2 * size, axis=axis),
    )


def columns_forward(re, im, turned):
    re, im = butterfly(re, im, 1.0)
    pairs = [
        halves(right_product(jnp.concatenate([a, b], axis=1), turned), 1) for a, b in zip(re, im)
    ]
    return jnp.concatenate([p[0] for p in pairs], axis=1), jnp.concatenate(
        [p[1] for p in pairs], axis=1
    )


def columns_inverse(re, im, plain):
    pairs = [
        halves(right_product(jnp.concatenate([a, b], axis=1), plain), 1)
        for a, b in zip(blocks_of(re, 1), blocks_of(im, 1))
    ]
    return butterfly([p[0] for p in pairs], [p[1] for p in pairs], -1.0)


def rows_forward(re, im, plain):
    re, im = butterfly(re, im, 1.0)
    pairs = [
        halves(left_product(plain, jnp.concatenate([a, b], axis=0)), 0) for a, b in zip(re, im)
    ]
    return jnp.concatenate([p[0] for p in pairs], axis=0), jnp.concatenate(
        [p[1] for p in pairs], axis=0
    )


def rows_inverse(re, im, turned):
    pairs = [
        halves(left_product(turned, jnp.concatenate([a, b], axis=0)), 0)
        for a, b in zip(blocks_of(re, 0), blocks_of(im, 0))
    ]
    return butterfly([p[0] for p in pairs], [p[1] for p in pairs], -1.0)


def rows_forward_real(blocks, plain):
    part = blocks[0].shape[0]
    total = blocks[1] + blocks[2]
    narrow = (plain[0][:, :part], plain[1][:, :part])
    first = halves(left_product(narrow, blocks[0] + total), 0)
    turned = jnp.concatenate(
        [blocks[0] - 0.5 * total, HALF_ROOT3 * (blocks[1] - blocks[2])], axis=0
    )
    second = halves(left_product(plain, turned), 0)
    return jnp.concatenate([first[0], second[0]], axis=0), jnp.concatenate(
        [first[1], second[1]], axis=0
    )


def rows_inverse_real(re, im, turned):
    re, im = blocks_of(re, 0), blocks_of(im, 0)
    part = re[0].shape[0]
    short = (turned[0][:part], turned[1][:part])
    base = left_product(short, jnp.concatenate([re[0], im[0]], axis=0))
    pair_re, pair_im = halves(left_product(turned, jnp.concatenate([re[1], im[1]], axis=0)), 0)
    near, far = base - pair_re, (2 * HALF_ROOT3) * pair_im
    return [base + 2.0 * pair_re, near + far, near - far]


def sine_cosine(angle):
    quarter = jnp.floor(angle * np.float32(2 / np.pi) + 0.5)
    rest = angle - quarter * np.float32(1.5703125)
    rest = rest - quarter * np.float32(4.837512969970703125e-4)
    rest = rest - quarter * np.float32(7.549789948768648e-8)
    square = rest * rest
    sine = rest + rest * square * (
        -1.6666654611e-1 + square * (8.3321608736e-3 - 1.9515295891e-4 * square)
    )
    cosine = (
        1.0
        - 0.5 * square
        + square
        * square
        * (4.166664568298827e-2 + square * (-1.388731625493765e-3 + 2.443315711809948e-5 * square))
    )
    turn = quarter.astype(jnp.int32) & 3
    swap = (turn & 1) == 1
    out_sine = jnp.where(swap, cosine, sine)
    out_cosine = jnp.where(swap, sine, cosine)
    out_sine = jnp.where(turn >= 2, -out_sine, out_sine)
    out_cosine = jnp.where((turn == 1) | (turn == 2), -out_cosine, out_cosine)
    return out_sine, out_cosine


def object_kernel(window_ref, fh, fl, th, tl, re_ref, im_ref):
    plain, turned = (fh[...], fl[...]), (th[...], tl[...])
    extent = window_ref.shape[0]
    values = window_ref[...] * (1.0 / (extent * extent))
    re, im = rows_forward_real(to_residues(blocks_of(values, 0), 0), plain)
    re, im = columns_forward(
        to_residues(blocks_of(re, 1), 1), to_residues(blocks_of(im, 1), 1), turned
    )
    re_ref[...] = re
    im_ref[...] = im


def pair_gradient(phases, target, amplitude, object_re, object_im, plain, turned):
    win_size = phases.shape[0]
    extent = object_re.shape[1]
    naturals = win_size // LANES
    inverse_total = 1.0 / (extent * extent * jnp.sum(amplitude * amplitude))
    sine, cosine = sine_cosine(phases)
    pupil_re, pupil_im = amplitude * cosine, amplitude * sine

    def parts(values, axis):
        return to_residues(blocks_of(values, axis), axis)

    re, im = rows_forward(parts(pupil_re, 0), parts(pupil_im, 0), plain)
    far_re, far_im = columns_forward(parts(re, 1), parts(im, 1), turned)
    spread = (far_re * far_re + far_im * far_im) * inverse_total
    re, im = rows_forward_real(blocks_of(spread, 0), plain)
    re, im = columns_forward(blocks_of(re, 1), blocks_of(im, 1), turned)
    re, im = re * object_re - im * object_im, re * object_im + im * object_re
    re, im = columns_inverse(re, im, plain)
    re = jnp.concatenate(to_natural(re, 1, naturals), axis=1)
    im = jnp.concatenate(to_natural(im, 1, naturals), axis=1)
    model = jnp.concatenate(to_natural(rows_inverse_real(re, im, turned), 0, naturals), axis=0)
    residual = (model - target) * (win_size * extent / target.shape[0])
    re, im = rows_forward_real(parts(residual, 0), plain)
    re, im = columns_forward(parts(re, 1), parts(im, 1), turned)
    re, im = re * object_re + im * object_im, im * object_re - re * object_im
    re, im = columns_inverse(re, im, plain)
    spread_grad = jnp.concatenate(
        rows_inverse_real(jnp.concatenate(re, axis=1), jnp.concatenate(im, axis=1), turned), axis=0
    )
    re, im = columns_inverse(far_re * spread_grad, far_im * spread_grad, plain)
    re = jnp.concatenate(to_natural(re, 1, naturals), axis=1)
    im = jnp.concatenate(to_natural(im, 1, naturals), axis=1)
    re, im = rows_inverse(re, im, turned)
    back_re = jnp.concatenate(to_natural(re, 0, naturals), axis=0)
    back_im = jnp.concatenate(to_natural(im, 0, naturals), axis=0)
    return 2.0 * inverse_total * (pupil_re * back_im - pupil_im * back_re)


def aligned(offset, unit, size, width):
    begin = jnp.minimum((offset // unit) * unit, size - width)
    return pl.multiple_of(begin, unit), offset - begin


def patch_kernel(
    rows_ref, bands_ref, target_ref, amplitude_ref, ore_ref, oim_ref, fh, fl, th, tl, out_ref, sheet
):
    count, layers, tile, win_size = bands_ref.shape
    reach = win_size + SUBLANES
    plain, turned = (fh[...], fl[...]), (th[...], tl[...])
    phases = None
    corners = []
    for layer in range(layers):
        for holder in range(count):
            sheet[layer, pl.ds(holder * tile, tile), :] = bands_ref[holder, layer]
        begin, shift = aligned(rows_ref[layer], SUBLANES, count * tile, reach)
        corners.append((begin, shift))
        rows = sheet[layer, pl.ds(begin, reach), :]
        rows = pltpu.roll(rows, jnp.where(shift == 0, 0, reach - shift), 0)[:win_size]
        phases = rows if phases is None else phases + rows
    gradient = pair_gradient(
        phases, target_ref[...], amplitude_ref[...], ore_ref[...], oim_ref[...], plain, turned
    )
    padded = jnp.concatenate([gradient, jnp.zeros((SUBLANES, win_size), jnp.float32)], axis=0)
    for layer in range(layers):
        begin, shift = corners[layer]
        sheet[layer] = jnp.zeros((count * tile, win_size), jnp.float32)
        sheet[layer, pl.ds(begin, reach), :] = pltpu.roll(padded, shift, 0)
        for holder in range(count):
            out_ref[holder, layer] = sheet[layer, pl.ds(holder * tile, tile), :]


def cut_kernel(cols_ref, screens_ref, out_ref):
    layers, tile, screen_cols = screens_ref.shape
    count, _, _, win_size = out_ref.shape
    reach = win_size + LANES

    @pl.loop(0, count)
    def _(patch):
        for layer in range(layers):
            begin, shift = aligned(cols_ref[layer, patch], LANES, screen_cols, reach)
            cells = screens_ref[layer, :, pl.ds(begin, reach)]
            cells = pltpu.roll(cells, jnp.where(shift == 0, 0, reach - shift), 1)
            out_ref[patch, layer] = cells[:, :win_size]


def add_kernel(cols_ref, frame_ref, bands_ref, keep_ref, send_ref, sheet):
    count, layers, tile, win_size = bands_ref.shape
    screen_cols = sheet.shape[2]
    reach = win_size + LANES
    chunks, _, _, width = keep_ref.shape
    sheet[...] = jnp.zeros_like(sheet)

    @pl.loop(0, count)
    def _(patch):
        for layer in range(layers):
            begin, shift = aligned(cols_ref[layer, patch], LANES, screen_cols, reach)
            cells = jnp.concatenate(
                [bands_ref[patch, layer], jnp.zeros((tile, LANES), jnp.float32)], axis=1
            )
            sheet[layer, :, pl.ds(begin, reach)] += pltpu.roll(cells, shift, 1)

    bit = frame_ref[0] & 1
    for chunk in range(chunks):
        absolute = chunk ^ (frame_ref[0] // 2)
        for ref, low in ((keep_ref, bit), (send_ref, 1 - bit)):
            begin = pl.multiple_of((2 * absolute + low) * width, LANES)
            for layer in range(layers):
                ref[chunk, layer] = sheet[layer, :, pl.ds(begin, width)]


def greet(axis, peers):
    barrier = pltpu.get_barrier_semaphore()
    for peer in peers:
        pl.semaphore_signal(
            barrier, inc=1, device_id={axis: peer}, device_id_type=pl.DeviceIdType.MESH
        )
    pl.semaphore_wait(barrier, len(peers))


def remote(source, target, send_sem, recv_sem, axis, peer):
    return pltpu.make_async_remote_copy(
        src_ref=source,
        dst_ref=target,
        send_sem=send_sem,
        recv_sem=recv_sem,
        device_id={axis: peer},
        device_id_type=pl.DeviceIdType.MESH,
    )


def far_first(count):
    return sorted(range(1, count), key=lambda step: -min(step, count - step))


def exchange(count, in_ref, out_ref, send_sem, recv_sem, own_sem, edges=()):
    me = lax.axis_index("patch")
    steps = far_first(count)
    peers = {step: lax.rem(me + step, count) for step in steps}
    greet("patch", [peers[step] for step in steps])
    copies = []
    for number, (source, target, step) in enumerate(edges):
        place = count + number
        copies.append(
            remote(source, target, send_sem.at[place], recv_sem.at[place], "patch", peers[step])
        )
    for step in steps:
        copies.append(
            remote(
                in_ref.at[peers[step]],
                out_ref.at[me],
                send_sem.at[step],
                recv_sem.at[step],
                "patch",
                peers[step],
            )
        )
    own = pltpu.make_async_copy(in_ref.at[me], out_ref.at[me], own_sem)
    for copy in copies:
        copy.start()
    own.start()
    for copy in copies:
        copy.wait()
    own.wait()


def forward_kernel(
    count, in_ref, head_ref, tail_ref, out_ref, right_ref, left_ref, send_sem, recv_sem, own_sem
):
    edges = ((tail_ref, left_ref, 1), (head_ref, right_ref, count - 1))
    exchange(count, in_ref, out_ref, send_sem, recv_sem, own_sem, edges)


def return_kernel(count, in_ref, out_ref, send_sem, recv_sem, own_sem):
    exchange(count, in_ref, out_ref, send_sem, recv_sem, own_sem)


def frame_kernel(count, keep_ref, send_ref, out_ref, total, near, distant, *sems):
    near_send, near_recv, far_send, far_recv = sems
    me = lax.axis_index("frame")
    chunks, layers = keep_ref.shape[:2]
    levels = count.bit_length() - 1
    peers = [me + (1 << k) * (1 - 2 * lax.rem(me // (1 << k), 2)) for k in range(levels)]
    greet("frame", peers)
    zeros = {r: (r & -r).bit_length() for r in range(1, chunks)}
    order = sorted(zeros, key=zeros.get) + [0]
    first = {}
    for r in order:
        for layer in range(layers):
            sems = (near_send.at[r, layer], near_recv.at[r, layer])
            first[r, layer] = remote(
                send_ref.at[r, layer], near.at[r, layer], *sems, "frame", peers[0]
            )
            first[r, layer].start()
    later = {}
    for r in order:
        top = zeros.get(r, levels)
        for layer in range(layers):
            first[r, layer].wait()
            value = keep_ref[r, layer] + near[r, layer]
            for k in range(1, top):
                later[r ^ (1 << (k - 1)), layer].wait()
                value = value + distant[r ^ (1 << (k - 1)), layer]
            if r == 0:
                out_ref[layer] = value
            else:
                total[r, layer] = value
                sems = (far_send.at[r, layer], far_recv.at[r, layer])
                later[r, layer] = remote(
                    total.at[r, layer], distant.at[r, layer], *sems, "frame", peers[top]
                )
                later[r, layer].start()


def call(kernel, out_shape, specs, scratch=(), flops=0, moved=0):
    return pl.pallas_call(
        kernel,
        out_shape=out_shape,
        in_specs=specs,
        out_specs=jax.tree.map(lambda _: VMEM_SPEC, out_shape),
        scratch_shapes=list(scratch),
        cost_estimate=pl.CostEstimate(flops=flops, bytes_accessed=moved, transcendentals=0),
        compiler_params=pltpu.CompilerParams(vmem_limit_bytes=VMEM_LIMIT),
    )


def talk(kernel, out_shape, specs, out_spec, scratch, identity):
    return pl.pallas_call(
        kernel,
        out_shape=out_shape,
        in_specs=specs,
        out_specs=jax.tree.map(lambda _: out_spec, out_shape),
        scratch_shapes=list(scratch),
        compiler_params=pltpu.CompilerParams(
            vmem_limit_bytes=VMEM_LIMIT, collective_id=identity, has_side_effects=True
        ),
    )


def frame_total(keep, send):
    count = lax.axis_size("frame")
    chunks, layers = keep.shape[:2]
    buffers = [pltpu.VMEM(keep.shape, jnp.float32)] * 3
    sems = [pltpu.SemaphoreType.DMA((chunks, layers))] * 4
    return talk(
        functools.partial(frame_kernel, count),
        jax.ShapeDtypeStruct(keep.shape[1:], jnp.float32),
        [VMEM_SPEC] * 2,
        VMEM_SPEC,
        buffers + sems,
        2,
    )(keep, send)


def body(screens, row_offsets, col_offsets, amplitude, object_strip, observed):
    patch_count = lax.axis_size("patch")
    frame_count = lax.axis_size("frame")
    place = lax.axis_index("patch")
    frame_id = lax.axis_index("frame")
    layers, tile, screen_cols = screens.shape
    win_size = amplitude.shape[0]
    extent = object_strip.shape[0]
    width = screen_cols // frame_count
    float_of = lambda *shape: jax.ShapeDtypeStruct(shape, jnp.float32)
    matrices = [jnp.asarray(m) for m in transform_matrices(extent)]
    cols = lax.dynamic_index_in_dim(col_offsets, frame_id, 0, keepdims=False)
    rows = lax.dynamic_slice(row_offsets, (frame_id, 0, place), (1, layers, 1)).reshape(layers)

    bands = call(
        cut_kernel,
        float_of(patch_count, layers, tile, win_size),
        [SMEM_SPEC, VMEM_SPEC],
        moved=2 * screens.size * 4,
    )(cols, screens)
    any_spec = pl.BlockSpec(memory_space=pl.ANY)
    head = lax.slice_in_dim(object_strip, 0, HALO, axis=1)
    tail = lax.slice_in_dim(object_strip, object_strip.shape[1] - HALO, None, axis=1)
    edge = float_of(extent, HALO)
    exchange_scratch = [
        pltpu.SemaphoreType.DMA((patch_count + 2,)),
        pltpu.SemaphoreType.DMA((patch_count + 2,)),
        pltpu.SemaphoreType.DMA,
    ]
    received, right, left = talk(
        functools.partial(forward_kernel, patch_count),
        (float_of(*bands.shape), edge, edge),
        [any_spec] * 3,
        any_spec,
        exchange_scratch,
        0,
    )(bands, head, tail)
    right = jnp.where(place == patch_count - 1, 0.0, right)
    left = jnp.where(place == 0, 0.0, left)
    window = jnp.concatenate([object_strip, right, left], axis=1)
    window = jnp.concatenate([window[HALO:], window[:HALO]], axis=0)
    spectrum = float_of(2 * (extent // RADIX), extent)
    object_re, object_im = call(
        object_kernel, (spectrum, spectrum), [VMEM_SPEC] * 5, flops=3 * 10**9, moved=2 * 10**6
    )(window, *matrices)

    outgoing = call(
        patch_kernel,
        float_of(patch_count, layers, tile, win_size),
        [SMEM_SPEC] + [VMEM_SPEC] * 9,
        scratch=[pltpu.VMEM((layers, patch_count * tile, win_size), jnp.float32)],
        flops=10**10,
        moved=8 * 10**6,
    )(rows, received, observed[0], amplitude, object_re, object_im, *matrices)
    returned = talk(
        functools.partial(return_kernel, patch_count),
        float_of(*outgoing.shape),
        [any_spec],
        any_spec,
        exchange_scratch,
        1,
    )(outgoing)

    pieces = float_of(frame_count // 2, layers, tile, width)
    keep, send = call(
        add_kernel,
        (pieces, pieces),
        [SMEM_SPEC, SMEM_SPEC, VMEM_SPEC],
        scratch=[pltpu.VMEM((layers, tile, screen_cols), jnp.float32)],
        moved=8 * 10**6,
    )(cols, frame_id.reshape(1).astype(jnp.int32), returned)
    return frame_total(keep, send)


def solution(mesh):
    in_specs = (P(None, "patch", None), P(), P(), P(), P(None, "patch"), P("frame", None, "patch"))
    out_specs = P(None, "patch", "frame")
    return jax.shard_map(body, mesh=mesh, in_specs=in_specs, out_specs=out_specs, check_vma=False)
```
